128 devices in a mesh: trow: 8 (over z, core), tcol: 16 (over x, y).
Axes of the slice: x: 4, y: 4, z: 4, core: 2. Of those that a mesh axis runs over, the one named last changes fastest.
Arguments:
- inputs: bfloat16 [2048, 8192], P('tcol', 'trow'), may hold values from -6 to 6
- grad_out: bfloat16 [2048, 8192], P('tcol', 'trow'), may hold values from -6 to 6
- pre_act: bfloat16 [2048, 16384], P('trow', 'tcol'), may hold values from -8 to 8
- up_w: bfloat16 [8, 64, 512, 512], P('trow', 'tcol'), may hold values from -0.0625 to 0.0625
- up_noise: bfloat16 [8, 64, 512, 512], P('trow', 'tcol'), may hold values from -0.3984375 to 0.3984375
- down_w: bfloat16 [8, 64, 512, 512], P('trow', 'tcol'), may hold values from -0.046875 to 0.046875
- down_noise: bfloat16 [8, 64, 512, 512], P('trow', 'tcol'), may hold values from -0.3984375 to 0.3984375
- up_slot: int32 [8, 64], P('trow', 'tcol'), may hold values from -1 to 3, as said below
- down_slot: int32 [8, 64], P('trow', 'tcol'), may hold values from -1 to 3, as said below
Outputs:
- input_grad: bfloat16 [2048, 8192], P('tcol', 'trow')
- up_grad: float32 [8, 64, 512, 512], P('trow', 'tcol')
- down_grad: float32 [8, 64, 512, 512], P('trow', 'tcol')
The draws below stay inside these ranges and needn't reach their ends.
Inputs may be any that keep to these rules, and one draw needn't show every extreme that they name: Each device's 4 entries of up_slot name distinct local positions in rising order, followed by -1 for empty slots; every device keeps at least one tile, one device keeps all 4 and another exactly one. `down_slot`: as for up_slot, drawn independently.
All inputs are finite; a program needn't handle non-finite values.
Results may differ from the reference program's by a relative error of at most 0.033.
Values may be sent and summed in bfloat16 or wider, within the bound.
No kernel may reach another device: no remote copies, remote signals or barrier semaphores. Data moves between devices by JAX's collectives and lax.ppermute only.
A program may use at most 128 MiB of HBM per device.

```python
import jax
import jax.numpy as jnp
from jax import lax

TILE = 512
D = 8192
FF = 16384
TOKENS = 2048
RT_DEV = 2
CT_DEV = 2
SLOTS = 4
N_TROW = 8
N_TCOL = 16


def slot_lists(key):
    devices = N_TROW * N_TCOL
    keys = jax.random.split(key, 5)
    first = jax.random.randint(keys[0], (devices,), 1, SLOTS + 1)
    second = jax.random.randint(keys[1], (devices,), 1, SLOTS + 1)
    counts = jnp.minimum(first, second)
    full_device = jax.random.randint(keys[2], (), 0, devices)
    single_device = (full_device + jax.random.randint(keys[3], (), 1, devices)) % devices
    device_ids = jnp.arange(devices)
    counts = jnp.where(device_ids == full_device, SLOTS, counts)
    counts = jnp.where(device_ids == single_device, 1, counts)
    orders = jax.vmap(lambda sub: jax.random.permutation(sub, SLOTS))(jax.random.split(keys[4], devices))
    places = jnp.arange(SLOTS)[None, :]
    chosen = jnp.where(places < counts[:, None], orders, SLOTS)
    chosen = jnp.sort(chosen, axis=1)
    chosen = jnp.where(chosen == SLOTS, -1, chosen)
    return chosen.reshape(N_TROW, N_TCOL * SLOTS).astype(jnp.int32)


def draw_up_slot(key, part):
    key = jax.random.fold_in(key, 11)
    return slot_lists(key)


def draw_down_slot(key, part):
    key = jax.random.fold_in(key, 23)
    return slot_lists(key)


def steps_of(own_key, dims, cuts, least, top_value):
    def one(dim, blocks):
        steps = jax.random.uniform(jax.random.fold_in(jax.random.fold_in(own_key, 6), dim), (blocks,), jnp.float32, least / len(cuts), top_value / len(cuts))
        return jnp.repeat(jnp.exp(steps), dims[dim] // blocks).reshape((-1,) + (1,) * (len(dims) - dim - 1))

    level = one(*cuts[0])
    for cut in cuts[1:]:
        level = level * one(*cut)
    return level


def scatter_about(key, extent, scale, limit, pieces=(), kind=jnp.bfloat16):
    array = scale * jax.random.normal(key, extent, jnp.float32)
    if pieces:
        array = array * steps_of(key, extent, pieces, -0.22, 0.18)
    return jnp.clip(array, -limit, limit).astype(kind)


def setup_inputs(seed: int = 0) -> dict:
    streams_of = jax.random.split(jax.random.key(seed), 10)
    return {
        "inputs": scatter_about(streams_of[0], (TOKENS, D), 1.0, 6.0, ((0, 16), (1, 8))),
        "grad_out": scatter_about(streams_of[1], (TOKENS, D), 1.0, 6.0, ((0, 16), (1, 8))),
        "pre_act": scatter_about(streams_of[2], (TOKENS, FF), 1.5, 8.0, ((0, 8), (1, 16))),
        "up_w": scatter_about(streams_of[3], (N_TROW, N_TCOL * SLOTS, TILE, TILE), D ** -0.5, 0.0625, ((0, 8), (1, 16))),
        "up_noise": scatter_about(streams_of[4], (N_TROW, N_TCOL * SLOTS, TILE, TILE), 0.1, 0.3984375, ((0, 8), (1, 16))),
        "down_w": scatter_about(streams_of[5], (N_TROW, N_TCOL * SLOTS, TILE, TILE), FF ** -0.5, 0.046875, ((0, 8), (1, 16))),
        "down_noise": scatter_about(streams_of[6], (N_TROW, N_TCOL * SLOTS, TILE, TILE), 0.1, 0.3984375, ((0, 8), (1, 16))),
        "up_slot": draw_up_slot(jax.random.fold_in(streams_of[9], 71), 0),
        "down_slot": draw_down_slot(jax.random.fold_in(streams_of[9], 71), 0),
    }


def silu_slope(values):
    wide = values.astype(jnp.float32)
    sigma = jax.nn.sigmoid(wide)
    return sigma * (1.0 + wide * (1.0 - sigma))


def noisy_weights(stored, noise):
    return (stored.astype(jnp.float32) * (1.0 + noise.astype(jnp.float32))).astype(jnp.bfloat16)


def rounded_back(values):
    return lax.optimization_barrier(values.astype(jnp.bfloat16)).astype(jnp.float32)


def reference(inputs, grad_out, pre_act, up_w, up_noise, down_w, down_noise, up_slot, down_slot):
    activations = jax.nn.silu(pre_act.astype(jnp.float32)).astype(jnp.bfloat16)
    blocks = N_TCOL * SLOTS
    contract_rows = (((0,), (0,)), ((), ()))
    contract_cols = (((1,), (1,)), ((), ()))
    act_grad = jnp.zeros((TOKENS, FF), jnp.float32)
    down_blocks = []
    for i in range(N_TROW):
        def down_pass(partial_value, slot_id):
            position = down_slot[i, slot_id]

            def live_slot(partial_value):
                row_start = (i * RT_DEV + position // CT_DEV) * TILE
                col_start = ((slot_id // SLOTS) * CT_DEV + position % CT_DEV) * TILE
                factor = 1.0 + down_noise[i, slot_id].astype(jnp.float32)
                noisy = noisy_weights(down_w[i, slot_id], down_noise[i, slot_id])
                dy_panel = lax.dynamic_slice_in_dim(grad_out, row_start, TILE, 1)
                act_panel = lax.dynamic_slice_in_dim(activations, col_start, TILE, 1)
                addition = lax.dot_general(dy_panel, noisy, contract_cols, preferred_element_type=jnp.float32)
                previous = lax.dynamic_slice_in_dim(partial_value, col_start, TILE, 1)
                partial_value = lax.dynamic_update_slice_in_dim(partial_value, previous + addition, col_start, 1)
                weight_grad = lax.dot_general(act_panel, dy_panel, contract_rows, preferred_element_type=jnp.float32) * factor
                return partial_value, weight_grad

            def empty_slot(partial_value):
                return partial_value, jnp.zeros((TILE, TILE), jnp.float32)

            return lax.cond(position >= 0, live_slot, empty_slot, partial_value)

        partial_value, grads_row = lax.scan(down_pass, jnp.zeros((TOKENS, FF), jnp.float32), jnp.arange(blocks, dtype=jnp.int32))
        act_grad = act_grad + rounded_back(partial_value)
        down_blocks.append(grads_row)
    down_grad = jnp.stack(down_blocks, axis=0)
    hidden_grad = (act_grad * silu_slope(pre_act)).astype(jnp.bfloat16)

    input_sum = jnp.zeros((TOKENS, D), jnp.float32)
    up_blocks = []
    row_ids = jnp.repeat(jnp.arange(N_TROW, dtype=jnp.int32), SLOTS)
    for j in range(N_TCOL):
        slot_ids = (j * SLOTS + jnp.tile(jnp.arange(SLOTS, dtype=jnp.int32), N_TROW)).astype(jnp.int32)

        def up_pass(total, pair):
            row_id, slot_id = pair
            position = up_slot[row_id, slot_id]

            def live_slot(total):
                row_start = (row_id * RT_DEV + position // CT_DEV) * TILE
                col_start = (j * CT_DEV + position % CT_DEV) * TILE
                factor = 1.0 + up_noise[row_id, slot_id].astype(jnp.float32)
                noisy = noisy_weights(up_w[row_id, slot_id], up_noise[row_id, slot_id])
                x_panel = lax.dynamic_slice_in_dim(inputs, row_start, TILE, 1)
                grad_panel = lax.dynamic_slice_in_dim(hidden_grad, col_start, TILE, 1)
                addition = lax.dot_general(grad_panel, noisy, contract_cols, preferred_element_type=jnp.float32)
                previous = lax.dynamic_slice_in_dim(total, row_start, TILE, 1)
                total = lax.dynamic_update_slice_in_dim(total, previous + addition, row_start, 1)
                weight_grad = lax.dot_general(x_panel, grad_panel, contract_rows, preferred_element_type=jnp.float32) * factor
                return total, weight_grad

            def empty_slot(total):
                return total, jnp.zeros((TILE, TILE), jnp.float32)

            return lax.cond(position >= 0, live_slot, empty_slot, total)

        total, grads_col = lax.scan(up_pass, jnp.zeros((TOKENS, D), jnp.float32), (row_ids, slot_ids))
        input_sum = input_sum + rounded_back(total)
        up_blocks.append(grads_col.reshape(N_TROW, SLOTS, TILE, TILE))
    up_grad = jnp.concatenate(up_blocks, axis=1)
    return input_sum.astype(jnp.bfloat16), up_grad, down_grad
```

```python
import jax
import jax.numpy as jnp
from jax import lax
from jax.sharding import Mesh, PartitionSpec as P

CHUNKS = 1


def shift(value, axis, step):
    n = lax.axis_size(axis)
    return lax.ppermute(value, axis, [(i, (i + step) % n) for i in range(n)])


def put(buffer, value, starts):
    return lax.dynamic_update_slice(buffer, value, starts)


def take(array, index, axis=0):
    return lax.dynamic_index_in_dim(array, index, axis, keepdims=False)


def silu_slope(values):
    wide = values.astype(jnp.float32)
    sigma = jax.nn.sigmoid(wide)
    return sigma * (1.0 + wide * (1.0 - sigma))


def noisy_weights(stored, noise):
    return (stored.astype(jnp.float32) * (1.0 + noise.astype(jnp.float32))).astype(jnp.bfloat16)


def tile_at(stored, noise, slots, place):
    hit = slots == place
    index = jnp.argmax(hit)
    tile = noisy_weights(take(stored, index), take(noise, index))
    return jnp.where(jnp.any(hit), tile, jnp.zeros_like(tile))


def slot_grads(dense, noise, slots, rows_are_hidden):
    size = noise.shape[-1]
    grads = []
    for s in range(noise.shape[0]):
        place = jnp.maximum(slots[s], 0)
        feature, hidden = place // 2 * size, place % 2 * size
        starts = (hidden, feature) if rows_are_hidden else (feature, hidden)
        tile = lax.dynamic_slice(dense, starts, (size, size))
        grad = tile * (1.0 + noise[s].astype(jnp.float32))
        grads.append(jnp.where(slots[s] >= 0, grad, 0.0))
    return jnp.stack(grads)[None]


def dot(a, b, contract, kind):
    return lax.dot_general(a, b, (contract, ((), ())), preferred_element_type=jnp.float32).astype(kind)


def add_up(parts):
    total = parts[0].astype(jnp.float32)
    for part in parts[1:]:
        total = total + part.astype(jnp.float32)
    return total


def on_device(inputs, grad_out, pre_act, up_w, up_noise, down_w, down_noise, up_slot, down_slot):
    z, c, x, y = (lax.axis_index(a) for a in ("z", "c", "x", "y"))
    bf16 = jnp.bfloat16
    rows, feats = grad_out.shape
    hidden = pre_act.shape[1]
    half = rows // 2
    tk = half // CHUNKS
    up_slots, down_slots = up_slot[0], down_slot[0]

    halves = grad_out.reshape(2, half, feats)
    dy_own = take(halves, c)
    dy_sib = shift(take(halves, 1 - c), "c", 1)

    h_full = lax.all_gather(pre_act, ("z", "c"), axis=0, tiled=True).reshape(4, 4, 2, half, hidden)
    inputs_late, _ = lax.optimization_barrier((inputs, h_full))
    x_full = lax.all_gather(inputs_late, ("x", "y"), axis=0, tiled=True)

    d = [tile_at(down_w[0], down_noise[0], down_slots, p) for p in range(4)]
    down_own = jnp.concatenate(
        [jnp.concatenate([d[0], d[2]], 1), jnp.concatenate([d[1], d[3]], 1)], 0
    )
    u = [tile_at(up_w[0], up_noise[0], up_slots, p) for p in range(4)]
    up_own = jnp.concatenate(
        [jnp.concatenate([u[0], u[1]], 1), jnp.concatenate([u[2], u[3]], 1)], 0
    )
    down_both = jnp.concatenate([down_own, shift(down_own, "c", 1)], 1)
    up_both = jnp.concatenate([up_own, shift(up_own, "c", 1)], 0)

    def gather_line(value, axis, me):
        line = jnp.zeros((4,) + value.shape, value.dtype)
        line = put(line, value[None], (me, 0, 0))
        for step in (1, 3, 2):
            line = put(line, shift(value, axis, -step)[None], ((me + step) % 4, 0, 0))
        return line

    def gather_plane(own, sib):
        line_own = gather_line(own, "x", x)
        line_sib = gather_line(sib, "y", y)
        full = jnp.zeros((4, 4, tk, 2 * feats), bf16)
        full = put(full, line_own[:, None], (0, y, 0, 0))
        full = put(full, line_sib[None], (x, 0, 0, feats))
        for step in (1, 3, 2):
            full = put(full, shift(line_own, "y", -step)[:, None], (0, (y + step) % 4, 0, 0))
            full = put(full, shift(line_sib, "x", -step)[None], ((x + step) % 4, 0, 0, feats))
        return full

    def scatter_line(array, axis, me, array_axis):
        parts = [take(array, me, array_axis)]
        for step in (1, 3, 2):
            parts.append(shift(take(array, (me + step) % 4, array_axis), axis, step))
        return add_up(parts)

    dy_parts, hg_parts, out_own, out_sib = [], [], [], []
    for k in range(CHUNKS):
        cut = slice(k * tk, (k + 1) * tk)
        dy = gather_plane(dy_own[cut], dy_sib[cut])
        dy_parts.append(dy)
        partial = dot(dy.reshape(16 * tk, 2 * feats), down_both, ((1,), (1,)), bf16)
        summed = scatter_line(partial.reshape(4, 4 * tk, hidden), "z", z, 0)
        h_here = lax.dynamic_slice(h_full, (z, 0, c, k * tk, 0), (1, 4, 1, tk, hidden))
        hg = (summed * silu_slope(h_here.reshape(4 * tk, hidden))).astype(bf16)
        hg_all = gather_line(hg, "z", z)
        hg_parts.append(hg_all.reshape(4, 4, tk, hidden))
        part = dot(hg_all.reshape(16 * tk, hidden), up_both, ((1,), (1,)), bf16)
        part = part.reshape(4, 4, tk, 2 * feats)
        own = scatter_line(part[..., :feats], "x", x, 0).astype(bf16)
        sib = scatter_line(part[..., feats:], "y", y, 1).astype(bf16)
        out_own.append(scatter_line(own, "y", y, 0).astype(bf16))
        out_sib.append(scatter_line(sib, "x", x, 0).astype(bf16))

    join = lambda parts, axis: parts[0] if len(parts) == 1 else jnp.concatenate(parts, axis)
    mine, theirs = join(out_own, 0), join(out_sib, 0)
    input_grad = jnp.zeros((2, half, feats), bf16)
    input_grad = put(input_grad, mine[None], (c, 0, 0))
    input_grad = put(input_grad, shift(theirs, "c", 1)[None], (1 - c, 0, 0))
    input_grad = input_grad.reshape(rows, feats)

    def both_halves(own, sent, width):
        whole = jnp.zeros((4, 4, 2, half, width), bf16)
        whole = put(whole, own[:, :, None], (0, 0, c, 0, 0))
        whole = put(whole, shift(sent, "c", 1)[:, :, None], (0, 0, 1 - c, 0, 0))
        return whole.reshape(16 * rows, width)

    dy = join(dy_parts, 2)
    dy_full = both_halves(dy[..., :feats], dy[..., feats:], feats)
    activations = jax.nn.silu(h_full.astype(jnp.float32)).astype(bf16).reshape(16 * rows, hidden)
    down_dense = dot(activations, dy_full, ((0,), (0,)), jnp.float32)
    down_grad = slot_grads(down_dense, down_noise[0], down_slots, True)

    hg = join(hg_parts, 2)
    hg_full = both_halves(hg, hg, hidden)
    up_dense = dot(x_full, hg_full, ((0,), (0,)), jnp.float32)
    up_grad = slot_grads(up_dense, up_noise[0], up_slots, False)
    return input_grad, up_grad, down_grad


def solution(mesh):
    fine = Mesh(mesh.devices.reshape(4, 2, 4, 4), ("z", "c", "x", "y"))
    row, col = ("z", "c"), ("x", "y")
    in_specs = (P(col, row), P(col, row), P(row, col)) + (P(row, col),) * 6
    out_specs = (P(col, row), P(row, col), P(row, col))
    return jax.shard_map(
        on_device, mesh=fine, in_specs=in_specs, out_specs=out_specs, check_vma=False
    )
```

```python
import functools

import jax
import jax.numpy as jnp
from jax import lax
from jax.experimental import pallas as pl
from jax.experimental.pallas import tpu as pltpu
from jax.sharding import Mesh, PartitionSpec as P


PLANE = ("c", "x", "y")
GRADS_VMEM = 24 * 2**20


def along(step, value, is_first):
    pairs = []
    for c in range(2):
        for x in range(4):
            for y in range(4):
                to = ((x + step) % 4, y) if (c == 0) == is_first else (x, (y + step) % 4)
                pairs.append(((c * 4 + x) * 4 + y, (c * 4 + to[0]) * 4 + to[1]))
    return lax.ppermute(value, PLANE, pairs)


def plane(step, value):
    return along(step, value, False)


def exchange_first(value):
    lines = [[x * 4 + y for x in range(4)] for y in range(4)]
    lines += [[16 + x * 4 + y for y in range(4)] for x in range(4)]
    return lax.all_to_all(value, PLANE, 0, 0, axis_index_groups=lines, tiled=True)


def exchange_z(value):
    return lax.all_to_all(value, "z", 0, 0, tiled=True)


def four(value):
    return jnp.broadcast_to(value[None], (4,) + value.shape)


def swap(value):
    return lax.ppermute(value, "c", [(0, 1), (1, 0)])


def unsigned(starts):
    return [jnp.uint32(i) if isinstance(i, int) else i for i in starts]


def put(buffer, value, starts):
    return lax.dynamic_update_slice(buffer, value, unsigned(starts))


def take(array, index, axis=0):
    starts = [0] * array.ndim
    starts[axis] = index
    sizes = list(array.shape)
    sizes[axis] = 1
    return lax.squeeze(lax.dynamic_slice(array, unsigned(starts), sizes), (axis,))


def after(value, *others):
    return lax.optimization_barrier((value, *others))[0]


def silu_slope(values):
    wide = values.astype(jnp.float32)
    sigma = jax.nn.sigmoid(wide)
    return sigma * (1.0 + wide * (1.0 - sigma))


def weights_kernel(slots, stored, noise, out):
    place = pl.program_id(0)
    live = slots[0] == place
    for s in range(1, 4):
        live = live | (slots[s] == place)

    @pl.when(live)
    def _():
        wide = stored[0].astype(jnp.float32) * (1.0 + noise[0].astype(jnp.float32))
        out[...] = wide.astype(out.dtype)

    @pl.when(jnp.logical_not(live))
    def _():
        out[...] = jnp.zeros_like(out)


def dense_weights(slots, stored, noise, hidden_rows):
    size = stored.shape[-1]

    def held_at(place, slots):
        index = jnp.int32(0)
        for s in range(1, 4):
            index = index + jnp.where(slots[s] == place, s, 0)
        return index, 0, 0

    def out_at(place, slots):
        return (place % 2, place // 2) if hidden_rows else (place // 2, place % 2)

    tile = pl.BlockSpec((1, size, size), held_at)
    return pl.pallas_call(
        weights_kernel,
        grid_spec=pltpu.PrefetchScalarGridSpec(
            num_scalar_prefetch=1,
            grid=(4,),
            in_specs=[tile, tile],
            out_specs=pl.BlockSpec((size, size), out_at),
        ),
        out_shape=jax.ShapeDtypeStruct((2 * size, 2 * size), stored.dtype),
        cost_estimate=pl.CostEstimate(flops=8 * size * size, bytes_accessed=24 * size * size, transcendentals=0),
        name="dense_weights",
    )(slots, stored, noise)


def grads_kernel(down, n_left, slots, place_of, *refs):
    lefts, owns, others = refs[:n_left], refs[n_left : n_left + 2], refs[n_left + 2 : -5]
    noise, out, left, right, sems = refs[-5:]
    s = pl.program_id(0)
    size, width, rows = out.shape[1], left.shape[-1], left.shape[-2]
    tk = others[0].shape[2]
    core, x, y = place_of[0], place_of[1], place_of[2]
    place = slots[s]
    hidden = pl.ds(pl.multiple_of((place & 1) * size, size), size)
    feature = pl.ds(pl.multiple_of((place >> 1) * size, size), size)
    a, b = (hidden, feature) if down else (feature, hidden)

    def line_at(array, half, from_core, d):
        return array.at[half, :, (y + d) & 3] if from_core == 0 else array.at[half, (x + d) & 3]

    def copies(me, half):
        pairs = []
        if down:
            for source, of in zip(lefts, (me, 1 - me)):
                pairs.append((source.at[:, :, half], left.at[half, :, pl.ds(2 * of, 2)]))
        else:
            for d, source in enumerate(lefts):
                pairs.append((source.at[:, half], line_at(left, half, me, d)))
        for k in range(2):
            for d in range(4):
                source = (owns if half == me else others)[k].at[d, :, :, pl.ds(0, width)]
                pairs.append((source, line_at(right, half, half, d).at[:, pl.ds(k * tk, tk)]))
        first = half * 12
        return [pltpu.make_async_copy(*pair, sems.at[first + i]) for i, pair in enumerate(pairs)]

    @pl.when(s == 0)
    def _():
        for me in range(2):

            @pl.when(core == me)
            def _():
                for half in range(2):
                    for copy in copies(me, half):
                        copy.start()

    for half in range(2):

        @pl.when(s == 0)
        def _():
            for me in range(2):

                @pl.when(core == me)
                def _():
                    for copy in copies(me, half):
                        copy.wait()

            if down:

                @pl.loop(0, 16)
                def _(i):
                    wide = left[half, i >> 2, i & 3].astype(jnp.float32)
                    left[half, i >> 2, i & 3] = (wide * jax.nn.sigmoid(wide)).astype(left.dtype)

        @pl.when(place >= 0)
        def _():
            rows_first = (((0,), (0,)), ((), ()))
            more = lax.dot_general(
                left[half, :, :, :, a].reshape(16 * rows, size),
                right[half, :, :, :, b].reshape(16 * rows, size),
                rows_first,
                preferred_element_type=jnp.float32,
            )
            if half == 0:
                out[0] = more
            else:
                out[0] = (more + out[0]) * (1.0 + noise[0].astype(jnp.float32))

    @pl.when(place < 0)
    def _():
        out[...] = jnp.zeros_like(out)


def slot_grads(slots, place_of, lefts, owns, others, noise, down):
    rows, width = lefts[0].shape[-2:]
    size = noise.shape[-1]
    tile = pl.BlockSpec((1, size, size), lambda s, *_: (s, 0, 0))
    anywhere = pl.BlockSpec(memory_space=pl.ANY)
    whole = pltpu.VMEM((2, 4, 4, rows, width), noise.dtype)
    return pl.pallas_call(
        functools.partial(grads_kernel, down, len(lefts)),
        grid_spec=pltpu.PrefetchScalarGridSpec(
            num_scalar_prefetch=2,
            grid=(4,),
            in_specs=[anywhere] * (len(lefts) + len(owns) + len(others)) + [tile],
            out_specs=tile,
            scratch_shapes=[whole, whole, pltpu.SemaphoreType.DMA((24,))],
        ),
        out_shape=jax.ShapeDtypeStruct(noise.shape, jnp.float32),
        compiler_params=pltpu.CompilerParams(vmem_limit_bytes=GRADS_VMEM),
        cost_estimate=pl.CostEstimate(
            flops=8 * 32 * rows * size * size, bytes_accessed=14 * 2**20, transcendentals=0
        ),
        name="slot_grads",
    )(slots, place_of, *lefts, *owns, *others, noise)


def dot(a, b, contract, kind):
    return lax.dot_general(a, b, (contract, ((), ())), preferred_element_type=jnp.float32).astype(kind)


def add_up(parts):
    total = parts[0].astype(jnp.float32)
    for part in parts[1:]:
        total = total + part.astype(jnp.float32)
    return total


def on_device(inputs, grad_out, pre_act, up_w, up_noise, down_w, down_noise, up_slot, down_slot):
    z, c, x, y = (lax.axis_index(a).astype(jnp.uint32) for a in ("z", "c", "x", "y"))
    first, second = jnp.where(c == 0, x, y), jnp.where(c == 0, y, x)
    other_c = c ^ jnp.uint32(1)
    ahead = lambda index, d: (index + jnp.asarray(d, jnp.uint32)) & jnp.uint32(3)
    bf16 = jnp.bfloat16
    rows, feats = grad_out.shape
    hidden = pre_act.shape[1]
    half = rows // 2
    tk = half // 2
    up_slots, down_slots = up_slot[0], down_slot[0]
    place_of = jnp.stack([c, x, y]).astype(jnp.int32)

    def down_product(dy):
        return dot(dy.reshape(-1, 2 * feats), down_both, ((1,), (1,)), bf16).reshape(4, -1, hidden)

    def up_product(hg):
        return dot(hg.reshape(-1, hidden), up_both, ((1,), (1,)), bf16).reshape(4, 4, tk, 2 * feats)

    def sum_of_four(parts):
        return add_up([parts[i] for i in range(4)])

    def pieces_of(line):
        return [plane(-d, line) for d in (1, 2, 3)]

    halves = grad_out.reshape(2, half, feats)
    here = jnp.concatenate([take(halves, c), swap(take(halves, other_c)), inputs], 0)
    down_own = dense_weights(down_slots, after(down_w, here)[0], down_noise[0], True)
    line = put(jnp.zeros((4,) + here.shape, bf16), here[None], (first, 0, 0))
    for d in (1, 3, 2):
        line = put(line, after(along(-d, here, True), down_own)[None], (ahead(first, d), 0, 0))

    h_own = exchange_z(four(pre_act)).reshape(4, 2, 2, half, hidden)
    line_a = jnp.concatenate([line[:, :tk], line[:, half : half + tk]], 2)
    line_b = jnp.concatenate([line[:, tk:half], line[:, half + tk : rows]], 2)
    line_x = line[:, rows:]
    down_both = jnp.concatenate([down_own, swap(down_own)], 1)

    pieces_a = [line_a, *pieces_of(line_a)]
    line_b, line_x = lax.optimization_barrier((line_b, line_x, *pieces_a))[:2]
    dy_a = jnp.stack(pieces_a)
    partial_a = down_product(after(dy_a, line_x))

    parts_a = exchange_z(after(partial_a, h_own))
    up_own = dense_weights(up_slots, after(up_w, partial_a)[0], up_noise[0], False)
    up_both = jnp.concatenate([up_own, swap(up_own)], 0)

    h_other = swap(h_own)
    at = ahead(second, z)
    near = at < jnp.uint32(2)
    on_0 = jnp.where(near, take(h_own, at & jnp.uint32(1), 1)[:, 0], take(h_other, at & jnp.uint32(1), 1)[:, 0])
    on_1 = jnp.concatenate([take(h_other, at)[:, 1], take(h_own, at)[:, 1]], 0)
    h_mine = jnp.where(c == 0, on_0, on_1)

    def hidden_grad(parts, k):
        slope = silu_slope(h_mine[:, k * tk : (k + 1) * tk].reshape(4 * tk, hidden))
        return (sum_of_four(parts) * slope).astype(bf16)

    hg_a = hidden_grad(after(parts_a, up_own), 0)
    other_a = swap(after(dy_a, partial_a)[..., feats:])
    dy_b = jnp.stack([line_b, *pieces_of(line_b)])
    partial_b = down_product(dy_b)
    all_a = after(exchange_z(four(hg_a)), partial_b, other_a)
    line_x = after(line_x, hg_a, dy_b)
    x_lines = [line_x, *pieces_of(line_x)]

    parts_b = exchange_z(after(partial_b, all_a))
    out_a = up_product(all_a)
    hg_b = hidden_grad(after(parts_b, out_a, *x_lines), 1)
    other_b = swap(after(dy_b, out_a)[..., feats:])
    own_a, *sent_a = lax.optimization_barrier([out_a[d] for d in range(4)])
    sum_a = add_up([own_a] + [plane(d, sent_a[d - 1]) for d in (1, 2, 3)]).astype(bf16)
    all_b = after(exchange_z(four(hg_b)), other_b, sum_a)
    out_b = up_product(all_b)
    own_b, *sent_b = lax.optimization_barrier([out_b[d] for d in range(4)])
    mine_a = sum_of_four(exchange_first(after(sum_a, all_b)))
    down_grad = slot_grads(
        down_slots, place_of, [h_own, h_other], [dy_a, dy_b], [other_a, other_b], down_noise[0], True
    )
    hgs = [hg.reshape(4, 4, tk, hidden) for hg in (all_a, all_b)]
    other_hgs = [swap(hg) for hg in hgs]
    sent_b = [after(plane(d, sent_b[d - 1]), down_grad, mine_a, *other_hgs) for d in (1, 2, 3)]
    sum_b = add_up([own_b] + sent_b).astype(bf16)
    x_lines = [line_x.reshape(4, 2, half, feats) for line_x in x_lines]
    up_grad = slot_grads(up_slots, place_of, x_lines, hgs, other_hgs, up_noise[0], False)
    mine_b = sum_of_four(after(exchange_first(sum_b), up_grad))
    mine = jnp.concatenate([mine_a, mine_b], 0).astype(bf16)
    input_grad = jnp.zeros((2, half, feats), bf16)
    input_grad = put(input_grad, mine[None, :, :feats], (c, 0, 0))
    input_grad = put(input_grad, swap(mine[:, feats:])[None], (other_c, 0, 0))
    return input_grad.reshape(rows, feats), up_grad[None], down_grad[None]


def solution(mesh):
    fine = Mesh(mesh.devices.reshape(4, 2, 4, 4), ("z", "c", "x", "y"))
    row, col = ("z", "c"), ("x", "y")
    in_specs = (P(col, row), P(col, row), P(row, col)) + (P(row, col),) * 6
    out_specs = (P(col, row), P(row, col), P(row, col))
    return jax.shard_map(
        on_device, mesh=fine, in_specs=in_specs, out_specs=out_specs, check_vma=False
    )
```

```python
import functools

import jax
import jax.numpy as jnp
from jax import lax
from jax.experimental import pallas as pl
from jax.experimental.pallas import tpu as pltpu
from jax.sharding import Mesh, PartitionSpec as P


PLANE = ("c", "x", "y")
GRADS_VMEM = 46 * 2**20


def along(step, value, is_first):
    pairs = []
    for c in range(2):
        for x in range(4):
            for y in range(4):
                to = ((x + step) % 4, y) if (c == 0) == is_first else (x, (y + step) % 4)
                pairs.append(((c * 4 + x) * 4 + y, (c * 4 + to[0]) * 4 + to[1]))
    return lax.ppermute(value, PLANE, pairs)


def plane(step, value):
    return along(step, value, False)


def exchange_first(value):
    lines = [[x * 4 + y for x in range(4)] for y in range(4)]
    lines += [[16 + x * 4 + y for y in range(4)] for x in range(4)]
    return lax.all_to_all(value, PLANE, 0, 0, axis_index_groups=lines, tiled=True)


def exchange_z(value):
    return lax.all_to_all(value, "z", 0, 0, tiled=True)


def four(value):
    return jnp.broadcast_to(value[None], (4,) + value.shape)


def swap(value):
    return lax.ppermute(value, "c", [(0, 1), (1, 0)])


def unsigned(starts):
    return [jnp.uint32(i) if isinstance(i, int) else i for i in starts]


def put(buffer, value, starts):
    return lax.dynamic_update_slice(buffer, value, unsigned(starts))


def take(array, index, axis=0):
    starts = [0] * array.ndim
    starts[axis] = index
    sizes = list(array.shape)
    sizes[axis] = 1
    return lax.squeeze(lax.dynamic_slice(array, unsigned(starts), sizes), (axis,))


def after(value, *others):
    return lax.optimization_barrier((value, *others))[0]


def silu_slope(values):
    wide = values.astype(jnp.float32)
    sigma = jax.nn.sigmoid(wide)
    return sigma * (1.0 + wide * (1.0 - sigma))


def weights_kernel(slots, stored, noise, out):
    place = pl.program_id(0)
    live = slots[0] == place
    for s in range(1, 4):
        live = live | (slots[s] == place)

    @pl.when(live)
    def _():
        wide = stored[0].astype(jnp.float32) * (1.0 + noise[0].astype(jnp.float32))
        out[...] = wide.astype(out.dtype)

    @pl.when(jnp.logical_not(live))
    def _():
        out[...] = jnp.zeros_like(out)


def dense_weights(slots, stored, noise, hidden_rows):
    size = stored.shape[-1]

    def held_at(place, slots):
        index = jnp.int32(0)
        for s in range(1, 4):
            index = index + jnp.where(slots[s] == place, s, 0)
        return index, 0, 0

    def out_at(place, slots):
        return (place % 2, place // 2) if hidden_rows else (place // 2, place % 2)

    tile = pl.BlockSpec((1, size, size), held_at)
    return pl.pallas_call(
        weights_kernel,
        grid_spec=pltpu.PrefetchScalarGridSpec(
            num_scalar_prefetch=1,
            grid=(4,),
            in_specs=[tile, tile],
            out_specs=pl.BlockSpec((size, size), out_at),
        ),
        out_shape=jax.ShapeDtypeStruct((2 * size, 2 * size), stored.dtype),
        cost_estimate=pl.CostEstimate(flops=8 * size * size, bytes_accessed=24 * size * size, transcendentals=0),
        name="dense_weights",
    )(slots, stored, noise)


def grads_kernel(down, n_left, n_own, slots, place_of, *refs):
    lefts, owns, others = refs[:n_left], refs[n_left : n_left + n_own], refs[n_left + n_own : -5]
    noise, out, left, right, sems = refs[-5:]
    s = pl.program_id(0)
    size, width, rows = out.shape[1], left.shape[-1], left.shape[-2]
    tk = others[0].shape[-2]
    core, x, y = place_of[0], place_of[1], place_of[2]
    place = slots[s]
    hidden = pl.ds(pl.multiple_of((place & 1) * size, size), size)
    feature = pl.ds(pl.multiple_of((place >> 1) * size, size), size)
    a, b = (hidden, feature) if down else (feature, hidden)

    def line_at(array, half, from_core, d):
        return array.at[half, :, (y + d) & 3] if from_core == 0 else array.at[half, (x + d) & 3]

    def copies(me, half):
        pairs = []
        if down:
            for source, of in zip(lefts, (me, 1 - me)):
                pairs.append((source.at[:, :, half], left.at[half, :, pl.ds(2 * of, 2)]))
        else:
            for d, source in enumerate(lefts):
                pairs.append((source.at[:, half], line_at(left, half, me, d)))
        for k in range(2):
            for d in range(4):
                if half == me:
                    source = owns[4 * k + d].at[:, :, pl.ds(0, width)] if down else owns[k].at[d]
                else:
                    source = others[0].at[k, d] if len(others) == 1 else others[k].at[d]
                pairs.append((source, line_at(right, half, half, d).at[:, pl.ds(k * tk, tk)]))
        first = half * 12
        return [pltpu.make_async_copy(*pair, sems.at[first + i]) for i, pair in enumerate(pairs)]

    @pl.when(s == 0)
    def _():
        for me in range(2):

            @pl.when(core == me)
            def _():
                for half in range(2):
                    for copy in copies(me, half):
                        copy.start()

    for half in range(2):

        @pl.when(s == 0)
        def _():
            for me in range(2):

                @pl.when(core == me)
                def _():
                    for copy in copies(me, half):
                        copy.wait()

            if down:

                @pl.loop(0, 16)
                def _(i):
                    wide = left[half, i >> 2, i & 3].astype(jnp.float32)
                    left[half, i >> 2, i & 3] = (wide * jax.nn.sigmoid(wide)).astype(left.dtype)

        @pl.when(place >= 0)
        def _():
            rows_first = (((0,), (0,)), ((), ()))
            more = lax.dot_general(
                left[half, :, :, :, a].reshape(16 * rows, size),
                right[half, :, :, :, b].reshape(16 * rows, size),
                rows_first,
                preferred_element_type=jnp.float32,
            )
            if half == 0:
                out[0] = more
            else:
                out[0] = (more + out[0]) * (1.0 + noise[0].astype(jnp.float32))

    @pl.when(place < 0)
    def _():
        out[...] = jnp.zeros_like(out)


def slot_grads(slots, place_of, lefts, owns, others, noise, down):
    rows, width = lefts[0].shape[-2:]
    size = noise.shape[-1]
    tile = pl.BlockSpec((1, size, size), lambda s, *_: (s, 0, 0))
    anywhere = pl.BlockSpec(memory_space=pl.ANY)
    whole = pltpu.VMEM((2, 4, 4, rows, width), noise.dtype)
    return pl.pallas_call(
        functools.partial(grads_kernel, down, len(lefts), len(owns)),
        grid_spec=pltpu.PrefetchScalarGridSpec(
            num_scalar_prefetch=2,
            grid=(4,),
            in_specs=[anywhere] * (len(lefts) + len(owns) + len(others)) + [tile],
            out_specs=tile,
            scratch_shapes=[whole, whole, pltpu.SemaphoreType.DMA((24,))],
        ),
        out_shape=jax.ShapeDtypeStruct(noise.shape, jnp.float32),
        compiler_params=pltpu.CompilerParams(vmem_limit_bytes=GRADS_VMEM),
        cost_estimate=pl.CostEstimate(
            flops=8 * 32 * rows * size * size, bytes_accessed=14 * 2**20, transcendentals=0
        ),
        name="slot_grads",
    )(slots, place_of, *lefts, *owns, *others, noise)


def dot(a, b, contract, kind):
    return lax.dot_general(a, b, (contract, ((), ())), preferred_element_type=jnp.float32).astype(kind)


def add_up(parts):
    total = parts[0].astype(jnp.float32)
    for part in parts[1:]:
        total = total + part.astype(jnp.float32)
    return total


def on_device(inputs, grad_out, pre_act, up_w, up_noise, down_w, down_noise, up_slot, down_slot):
    z, c, x, y = (lax.axis_index(a).astype(jnp.uint32) for a in ("z", "c", "x", "y"))
    first, second = jnp.where(c == 0, x, y), jnp.where(c == 0, y, x)
    other_c = c ^ jnp.uint32(1)
    ahead = lambda index, d: (index + jnp.asarray(d, jnp.uint32)) & jnp.uint32(3)
    bf16 = jnp.bfloat16
    rows, feats = grad_out.shape
    hidden = pre_act.shape[1]
    half = rows // 2
    tk = half // 2
    up_slots, down_slots = up_slot[0], down_slot[0]
    place_of = jnp.stack([c, x, y]).astype(jnp.int32)

    def down_product(dy):
        return dot(dy.reshape(-1, 2 * feats), down_both, ((1,), (1,)), bf16).reshape(4, -1, hidden)

    def up_product(hg):
        return dot(hg.reshape(-1, hidden), up_both, ((1,), (1,)), bf16).reshape(4, 4, tk, 2 * feats)

    def sum_of_four(parts):
        return add_up([parts[i] for i in range(4)])

    def pieces_of(line):
        return [plane(-d, line) for d in (1, 2, 3)]

    def line_of(pieces):
        line = jnp.zeros((4,) + pieces[0].shape, bf16)
        for d, piece in enumerate(pieces):
            line = put(line, piece[None], (ahead(first, d), 0, 0))
        return line

    halves, other_halves = (rows_of.reshape(2, half, feats) for rows_of in (grad_out, swap(grad_out)))
    here = jnp.concatenate([take(halves, c), take(other_halves, c), inputs], 0)
    down_own = dense_weights(down_slots, after(down_w, here)[0], down_noise[0], True)
    near = [here] + [after(along(-d, here, True), down_own) for d in (1, 2, 3)]
    both = lambda piece, cut: jnp.concatenate([piece[:half][cut], piece[half:rows][cut]], 1)
    line_a = line_of([both(piece, slice(0, tk)) for piece in near])
    line_b = line_of([both(piece, slice(tk, half)) for piece in near])
    line_x = line_of([after(piece, line_a)[rows:] for piece in near])

    h_own = exchange_z(four(after(pre_act, here))).reshape(4, 2, 2, half, hidden)
    down_both = jnp.concatenate([down_own, swap(down_own)], 1)

    up_own = dense_weights(up_slots, after(up_w, line_a)[0], up_noise[0], False)
    pieces_a = [line_a, *pieces_of(line_a)]
    dy_a = jnp.stack(pieces_a)
    partial_a = down_product(after(dy_a, line_x, up_own))

    parts_a = exchange_z(after(partial_a, h_own))
    up_both = jnp.concatenate([up_own, swap(up_own)], 0)

    h_other = swap(after(h_own, partial_a))
    h_here = after(h_own, h_other)
    at = ahead(second, z)
    near = at < jnp.uint32(2)
    on_0 = jnp.where(near, take(h_here, at & jnp.uint32(1), 1)[:, 0], take(h_other, at & jnp.uint32(1), 1)[:, 0])
    on_1 = jnp.concatenate([take(h_other, at)[:, 1], take(h_here, at)[:, 1]], 0)
    h_mine = jnp.where(c == 0, on_0, on_1)

    def hidden_grad(parts, k):
        return (sum_of_four(parts) * slopes[k].reshape(4 * tk, hidden)).astype(bf16)

    slopes = silu_slope(h_mine)
    slopes = lax.optimization_barrier([slopes[:, :tk], slopes[:, tk:]])

    other_a = swap(after(dy_a, h_other)[..., feats:])
    hg_a = hidden_grad(after(parts_a, other_a, *slopes), 0)
    line_b = after(line_b, h_other, *pieces_a)
    pieces_b = [line_b, *pieces_of(line_b)]
    dy_b = jnp.stack(pieces_b)
    other_b = swap(dy_b[..., feats:])
    partial_b = down_product(dy_b)
    sent_b = after(partial_b, other_b)
    parts_b = [take(partial_b, z)]
    for d in (1, 2, 3):
        parts_b.append(lax.ppermute(take(sent_b, ahead(z, d)), "z", [(i, (i + d) % 4) for i in range(4)]))
    all_a = after(exchange_z(four(hg_a)), partial_b)

    line_x = after(line_x, hg_a, dy_b)
    x_1, x_3 = plane(-1, line_x), plane(-3, line_x)
    x_2 = plane(-2, after(line_x, x_1, x_3))
    down_grad = slot_grads(
        down_slots, place_of, [h_own, h_other], pieces_a + pieces_b, [other_a, other_b], down_noise[0], True
    )
    hg_b = hidden_grad([after(parts_b[0], all_a, down_grad, x_1, x_3)] + parts_b[1:], 1)
    out_a = up_product(after(all_a, hg_b))
    own_a, *sent_a = lax.optimization_barrier([out_a[d] for d in range(4)])
    sum_a = add_up([own_a] + [plane(d, sent_a[d - 1]) for d in (1, 2, 3)]).astype(bf16)
    hgs = [hg.reshape(4, 4, tk, hidden) for hg in (all_a, exchange_z(four(hg_b)))]
    other_hg = swap(hgs[0])
    all_b = after(hgs[1], other_hg, x_2, *sent_a)
    out_b = up_product(all_b)
    own_b, *sent_b = lax.optimization_barrier([out_b[d] for d in range(4)])
    x_lines = [line_x.reshape(4, 2, half, feats) for line_x in (line_x, x_1, x_2, x_3)]
    up_grad = slot_grads(up_slots, place_of, x_lines, [hgs[0], all_b], [other_hg, swap(all_b)], up_noise[0], False)
    sum_b = add_up([own_b] + [after(plane(d, sent_b[d - 1]), up_grad) for d in (1, 2, 3)]).astype(bf16)
    summed = exchange_first(jnp.concatenate([sum_a, sum_b], 1))
    mine = sum_of_four(summed).astype(bf16)
    input_grad = jnp.zeros((2, half, feats), bf16)
    input_grad = put(input_grad, mine[None, :, :feats], (c, 0, 0))
    input_grad = put(input_grad, swap(mine[:, feats:])[None], (other_c, 0, 0))
    return input_grad.reshape(rows, feats), up_grad[None], down_grad[None]


def solution(mesh):
    fine = Mesh(mesh.devices.reshape(4, 2, 4, 4), ("z", "c", "x", "y"))
    row, col = ("z", "c"), ("x", "y")
    in_specs = (P(col, row), P(col, row), P(row, col)) + (P(row, col),) * 6
    out_specs = (P(col, row), P(row, col), P(row, col))
    return jax.shard_map(
        on_device, mesh=fine, in_specs=in_specs, out_specs=out_specs, check_vma=False
    )
```

```python
import functools

import jax
import jax.numpy as jnp
from jax import lax
from jax.experimental import pallas as pl
from jax.experimental.pallas import tpu as pltpu
from jax.sharding import Mesh, PartitionSpec as P


PLANE = ("c", "x", "y")
GRADS_VMEM = 46 * 2**20


def along(step, value, is_first):
    pairs = []
    for c in range(2):
        for x in range(4):
            for y in range(4):
                to = ((x + step) % 4, y) if (c == 0) == is_first else (x, (y + step) % 4)
                pairs.append(((c * 4 + x) * 4 + y, (c * 4 + to[0]) * 4 + to[1]))
    return lax.ppermute(value, PLANE, pairs)


def plane(step, value):
    return along(step, value, False)


def exchange_first(value):
    lines = [[x * 4 + y for x in range(4)] for y in range(4)]
    lines += [[16 + x * 4 + y for y in range(4)] for x in range(4)]
    return lax.all_to_all(value, PLANE, 0, 0, axis_index_groups=lines, tiled=True)


def exchange_z(value):
    return lax.all_to_all(value, "z", 0, 0, tiled=True)


def four(value):
    return jnp.broadcast_to(value[None], (4,) + value.shape)


def swap(value):
    return lax.ppermute(value, "c", [(0, 1), (1, 0)])


def unsigned(starts):
    return [jnp.uint32(i) if isinstance(i, int) else i for i in starts]


def put(buffer, value, starts):
    return lax.dynamic_update_slice(buffer, value, unsigned(starts))


def take(array, index, axis=0):
    starts = [0] * array.ndim
    starts[axis] = index
    sizes = list(array.shape)
    sizes[axis] = 1
    return lax.squeeze(lax.dynamic_slice(array, unsigned(starts), sizes), (axis,))


def after(value, *others):
    return lax.optimization_barrier((value, *others))[0]


def in_turn(value, *others):
    anywhere = pl.BlockSpec(memory_space=pl.ANY)
    return pl.pallas_call(
        lambda *refs: None,
        in_specs=[anywhere] * (1 + len(others)),
        out_specs=anywhere,
        out_shape=jax.ShapeDtypeStruct(value.shape, value.dtype),
        input_output_aliases={0: 0},
        cost_estimate=pl.CostEstimate(flops=0, bytes_accessed=0, transcendentals=0),
        name="in_turn",
    )(value, *others)


def silu_slope(values):
    wide = values.astype(jnp.float32)
    sigma = jax.nn.sigmoid(wide)
    return sigma * (1.0 + wide * (1.0 - sigma))


def weights_kernel(slots, stored, noise, out):
    place = pl.program_id(0)
    live = slots[0] == place
    for s in range(1, 4):
        live = live | (slots[s] == place)

    @pl.when(live)
    def _():
        wide = stored[0].astype(jnp.float32) * (1.0 + noise[0].astype(jnp.float32))
        out[...] = wide.astype(out.dtype)

    @pl.when(jnp.logical_not(live))
    def _():
        out[...] = jnp.zeros_like(out)


def dense_weights(slots, stored, noise, hidden_rows):
    size = stored.shape[-1]

    def held_at(place, slots):
        index = jnp.int32(0)
        for s in range(1, 4):
            index = index + jnp.where(slots[s] == place, s, 0)
        return index, 0, 0

    def out_at(place, slots):
        return (place % 2, place // 2) if hidden_rows else (place // 2, place % 2)

    tile = pl.BlockSpec((1, size, size), held_at)
    return pl.pallas_call(
        weights_kernel,
        grid_spec=pltpu.PrefetchScalarGridSpec(
            num_scalar_prefetch=1,
            grid=(4,),
            in_specs=[tile, tile],
            out_specs=pl.BlockSpec((size, size), out_at),
        ),
        out_shape=jax.ShapeDtypeStruct((2 * size, 2 * size), stored.dtype),
        cost_estimate=pl.CostEstimate(flops=8 * size * size, bytes_accessed=24 * size * size, transcendentals=0),
        name="dense_weights",
    )(slots, stored, noise)


def grads_kernel(down, n_left, n_own, slots, place_of, *refs):
    lefts, owns, others = refs[:n_left], refs[n_left : n_left + n_own], refs[n_left + n_own : -5]
    noise, out, left, right, sems = refs[-5:]
    s = pl.program_id(0)
    size, width, rows = out.shape[1], left.shape[-1], left.shape[-2]
    tk = others[0].shape[-2]
    core, x, y = place_of[0], place_of[1], place_of[2]
    place = slots[s]
    hidden = pl.ds(pl.multiple_of((place & 1) * size, size), size)
    feature = pl.ds(pl.multiple_of((place >> 1) * size, size), size)
    a, b = (hidden, feature) if down else (feature, hidden)

    def line_at(array, half, from_core, d):
        return array.at[half, :, (y + d) & 3] if from_core == 0 else array.at[half, (x + d) & 3]

    def copies(me, half):
        pairs = []
        if down:
            for source, of in zip(lefts, (me, 1 - me)):
                pairs.append((source.at[:, :, half], left.at[half, :, pl.ds(2 * of, 2)]))
        else:
            for d, source in enumerate(lefts):
                pairs.append((source.at[:, half], line_at(left, half, me, d)))
        for k in range(2):
            for d in range(4):
                if half == me:
                    source = owns[4 * k + d].at[:, :, pl.ds(0, width)] if down else owns[k].at[d]
                else:
                    source = others[0].at[k, d] if len(others) == 1 else others[k].at[d]
                pairs.append((source, line_at(right, half, half, d).at[:, pl.ds(k * tk, tk)]))
        first = half * 12
        return [pltpu.make_async_copy(*pair, sems.at[first + i]) for i, pair in enumerate(pairs)]

    @pl.when(s == 0)
    def _():
        for me in range(2):

            @pl.when(core == me)
            def _():
                for half in range(2):
                    for copy in copies(me, half):
                        copy.start()

    for half in range(2):

        @pl.when(s == 0)
        def _():
            for me in range(2):

                @pl.when(core == me)
                def _():
                    for copy in copies(me, half):
                        copy.wait()

            if down:

                @pl.loop(0, 16)
                def _(i):
                    wide = left[half, i >> 2, i & 3].astype(jnp.float32)
                    left[half, i >> 2, i & 3] = (wide * jax.nn.sigmoid(wide)).astype(left.dtype)

        @pl.when(place >= 0)
        def _():
            rows_first = (((0,), (0,)), ((), ()))
            more = lax.dot_general(
                left[half, :, :, :, a].reshape(16 * rows, size),
                right[half, :, :, :, b].reshape(16 * rows, size),
                rows_first,
                preferred_element_type=jnp.float32,
            )
            if half == 0:
                out[0] = more
            else:
                out[0] = (more + out[0]) * (1.0 + noise[0].astype(jnp.float32))

    @pl.when(place < 0)
    def _():
        out[...] = jnp.zeros_like(out)


def slot_grads(slots, place_of, lefts, owns, others, noise, down):
    rows, width = lefts[0].shape[-2:]
    size = noise.shape[-1]
    tile = pl.BlockSpec((1, size, size), lambda s, *_: (s, 0, 0))
    anywhere = pl.BlockSpec(memory_space=pl.ANY)
    whole = pltpu.VMEM((2, 4, 4, rows, width), noise.dtype)
    return pl.pallas_call(
        functools.partial(grads_kernel, down, len(lefts), len(owns)),
        grid_spec=pltpu.PrefetchScalarGridSpec(
            num_scalar_prefetch=2,
            grid=(4,),
            in_specs=[anywhere] * (len(lefts) + len(owns) + len(others)) + [tile],
            out_specs=tile,
            scratch_shapes=[whole, whole, pltpu.SemaphoreType.DMA((24,))],
        ),
        out_shape=jax.ShapeDtypeStruct(noise.shape, jnp.float32),
        compiler_params=pltpu.CompilerParams(vmem_limit_bytes=GRADS_VMEM),
        cost_estimate=pl.CostEstimate(
            flops=8 * 32 * rows * size * size, bytes_accessed=14 * 2**20, transcendentals=0
        ),
        name="slot_grads",
    )(slots, place_of, *lefts, *owns, *others, noise)


def dot(a, b, contract, kind):
    return lax.dot_general(a, b, (contract, ((), ())), preferred_element_type=jnp.float32).astype(kind)


def add_up(parts):
    total = parts[0].astype(jnp.float32)
    for part in parts[1:]:
        total = total + part.astype(jnp.float32)
    return total


def on_device(inputs, grad_out, pre_act, up_w, up_noise, down_w, down_noise, up_slot, down_slot):
    z, c, x, y = (lax.axis_index(a).astype(jnp.uint32) for a in ("z", "c", "x", "y"))
    first, second = jnp.where(c == 0, x, y), jnp.where(c == 0, y, x)
    other_c = c ^ jnp.uint32(1)
    ahead = lambda index, d: (index + jnp.asarray(d, jnp.uint32)) & jnp.uint32(3)
    bf16 = jnp.bfloat16
    rows, feats = grad_out.shape
    hidden = pre_act.shape[1]
    half = rows // 2
    tk = half // 2
    up_slots, down_slots = up_slot[0], down_slot[0]
    place_of = jnp.stack([c, x, y]).astype(jnp.int32)

    def down_product(dy):
        return dot(dy.reshape(-1, 2 * feats), down_both, ((1,), (1,)), bf16).reshape(4, -1, hidden)

    def up_product(hg):
        return dot(hg.reshape(-1, hidden), up_both, ((1,), (1,)), bf16).reshape(4, 4, tk, 2 * feats)

    def sum_of_four(parts):
        return add_up([parts[i] for i in range(4)])

    def pieces_of(line):
        return [plane(-d, line) for d in (1, 2, 3)]

    def line_of(pieces):
        line = jnp.zeros((4,) + pieces[0].shape, bf16)
        for d, piece in enumerate(pieces):
            line = put(line, piece[None], (ahead(first, d), 0, 0))
        return line

    halves, other_halves = (rows_of.reshape(2, half, feats) for rows_of in (grad_out, swap(grad_out)))
    here = jnp.concatenate([take(halves, c), take(other_halves, c), inputs], 0)
    down_own = dense_weights(down_slots, after(down_w, here)[0], down_noise[0], True)
    near = [here] + [after(along(-d, here, True), down_own) for d in (1, 2, 3)]
    both = lambda piece, cut: jnp.concatenate([piece[:half][cut], piece[half:rows][cut]], 1)
    line_a = line_of([both(piece, slice(0, tk)) for piece in near])
    line_b = line_of([both(piece, slice(tk, half)) for piece in near])
    line_x = line_of([after(piece, line_a)[rows:] for piece in near])

    h_own = exchange_z(four(after(pre_act, here))).reshape(4, 2, 2, half, hidden)
    down_both = jnp.concatenate([down_own, swap(down_own)], 1)

    up_own = dense_weights(up_slots, after(up_w, line_a)[0], up_noise[0], False)
    pieces_a = [line_a, *pieces_of(line_a)]
    dy_a = jnp.stack(pieces_a)
    partial_a = down_product(after(dy_a, line_x, up_own))

    parts_a = exchange_z(after(partial_a, h_own))
    up_both = jnp.concatenate([up_own, swap(up_own)], 0)

    h_other = swap(after(h_own, partial_a))
    h_here = after(h_own, h_other)
    at = ahead(second, z)
    near = at < jnp.uint32(2)
    on_0 = jnp.where(near, take(h_here, at & jnp.uint32(1), 1)[:, 0], take(h_other, at & jnp.uint32(1), 1)[:, 0])
    on_1 = jnp.concatenate([take(h_other, at)[:, 1], take(h_here, at)[:, 1]], 0)
    h_mine = jnp.where(c == 0, on_0, on_1)

    def hidden_grad(parts, k):
        return (sum_of_four(parts) * slopes[k].reshape(4 * tk, hidden)).astype(bf16)

    slopes = silu_slope(h_mine)
    slopes = lax.optimization_barrier([slopes[:, :tk], slopes[:, tk:]])

    other_a = swap(after(dy_a, h_other)[..., feats:])
    hg_a = hidden_grad(after(parts_a, other_a, *slopes), 0)
    line_b = after(line_b, h_other, *pieces_a)
    pieces_b = [line_b, *pieces_of(line_b)]
    dy_b = jnp.stack(pieces_b)
    other_b = swap(dy_b[..., feats:])
    partial_b = down_product(dy_b)
    sent_b = after(partial_b, other_b)
    parts_b = [take(partial_b, z)]
    for d in (1, 2, 3):
        parts_b.append(lax.ppermute(take(sent_b, ahead(z, d)), "z", [(i, (i + d) % 4) for i in range(4)]))
    sent_hg = four(hg_a)
    all_a = after(exchange_z(sent_hg), partial_b)

    line_x = in_turn(line_x, sent_hg)
    x_1, x_3 = plane(-1, line_x), plane(-3, line_x)
    x_2 = plane(-2, after(line_x, x_1, x_3))
    down_grad = slot_grads(
        down_slots, place_of, [h_own, h_other], pieces_a + pieces_b, [other_a, other_b], down_noise[0], True
    )
    hg_b = hidden_grad([after(parts_b[0], all_a, down_grad)] + parts_b[1:], 1)
    out_a = up_product(after(all_a, hg_b))
    own_a, *sent_a = lax.optimization_barrier([out_a[d] for d in range(4)])
    sum_a = add_up([own_a] + [plane(d, sent_a[d - 1]) for d in (1, 2, 3)]).astype(bf16)
    hgs = [hg.reshape(4, 4, tk, hidden) for hg in (all_a, exchange_z(four(hg_b)))]
    other_hg = swap(hgs[0])
    all_b = after(hgs[1], other_hg, x_2, *sent_a)
    out_b = up_product(all_b)
    own_b, *sent_b = lax.optimization_barrier([out_b[d] for d in range(4)])
    x_lines = [line_x.reshape(4, 2, half, feats) for line_x in (line_x, x_1, x_2, x_3)]
    up_grad = slot_grads(up_slots, place_of, x_lines, [hgs[0], all_b], [other_hg, swap(all_b)], up_noise[0], False)
    sum_b = add_up([own_b] + [after(plane(d, sent_b[d - 1]), up_grad) for d in (1, 2, 3)]).astype(bf16)
    summed = exchange_first(jnp.concatenate([sum_a, sum_b], 1))
    mine = sum_of_four(summed).astype(bf16)
    input_grad = jnp.zeros((2, half, feats), bf16)
    input_grad = put(input_grad, mine[None, :, :feats], (c, 0, 0))
    input_grad = put(input_grad, swap(mine[:, feats:])[None], (other_c, 0, 0))
    return input_grad.reshape(rows, feats), up_grad[None], down_grad[None]


def solution(mesh):
    fine = Mesh(mesh.devices.reshape(4, 2, 4, 4), ("z", "c", "x", "y"))
    row, col = ("z", "c"), ("x", "y")
    in_specs = (P(col, row), P(col, row), P(row, col)) + (P(row, col),) * 6
    out_specs = (P(col, row), P(row, col), P(row, col))
    return jax.shard_map(
        on_device, mesh=fine, in_specs=in_specs, out_specs=out_specs, check_vma=False
    )
```

```python
import functools

import jax
import jax.numpy as jnp
from jax import lax
from jax.experimental import pallas as pl
from jax.experimental.pallas import tpu as pltpu
from jax.sharding import Mesh, PartitionSpec as P


PLANE = ("c", "x", "y")
GRADS_VMEM = 46 * 2**20


def along(step, value, is_first):
    pairs = []
    for c in range(2):
        for x in range(4):
            for y in range(4):
                to = ((x + step) % 4, y) if (c == 0) == is_first else (x, (y + step) % 4)
                pairs.append(((c * 4 + x) * 4 + y, (c * 4 + to[0]) * 4 + to[1]))
    return lax.ppermute(value, PLANE, pairs)


def plane(step, value):
    return along(step, value, False)


def exchange_first(value):
    lines = [[x * 4 + y for x in range(4)] for y in range(4)]
    lines += [[16 + x * 4 + y for y in range(4)] for x in range(4)]
    return lax.all_to_all(value, PLANE, 0, 0, axis_index_groups=lines, tiled=True)


def exchange_z(value):
    return lax.all_to_all(value, "z", 0, 0, tiled=True)


def four(value):
    return jnp.broadcast_to(value[None], (4,) + value.shape)


def swap(value):
    return lax.ppermute(value, "c", [(0, 1), (1, 0)])


def unsigned(starts):
    return [jnp.uint32(i) if isinstance(i, int) else i for i in starts]


def put(buffer, value, starts):
    return lax.dynamic_update_slice(buffer, value, unsigned(starts))


def take(array, index, axis=0):
    starts = [0] * array.ndim
    starts[axis] = index
    sizes = list(array.shape)
    sizes[axis] = 1
    return lax.squeeze(lax.dynamic_slice(array, unsigned(starts), sizes), (axis,))


def after(value, *others):
    return lax.optimization_barrier((value, *others))[0]


def in_turn(value, *others):
    anywhere = pl.BlockSpec(memory_space=pl.ANY)
    return pl.pallas_call(
        lambda *refs: None,
        in_specs=[anywhere] * (1 + len(others)),
        out_specs=anywhere,
        out_shape=jax.ShapeDtypeStruct(value.shape, value.dtype),
        input_output_aliases={0: 0},
        cost_estimate=pl.CostEstimate(flops=0, bytes_accessed=0, transcendentals=0),
        name="in_turn",
    )(value, *others)


def silu_slope(values):
    wide = values.astype(jnp.float32)
    sigma = jax.nn.sigmoid(wide)
    return sigma * (1.0 + wide * (1.0 - sigma))


def weights_kernel(slots, stored, noise, out):
    place = pl.program_id(0)
    live = slots[0] == place
    for s in range(1, 4):
        live = live | (slots[s] == place)

    @pl.when(live)
    def _():
        wide = stored[0].astype(jnp.float32) * (1.0 + noise[0].astype(jnp.float32))
        out[...] = wide.astype(out.dtype)

    @pl.when(jnp.logical_not(live))
    def _():
        out[...] = jnp.zeros_like(out)


def dense_weights(slots, stored, noise, hidden_rows):
    size = stored.shape[-1]

    def held_at(place, slots):
        index = jnp.int32(0)
        for s in range(1, 4):
            index = index + jnp.where(slots[s] == place, s, 0)
        return index, 0, 0

    def out_at(place, slots):
        return (place % 2, place // 2) if hidden_rows else (place // 2, place % 2)

    tile = pl.BlockSpec((1, size, size), held_at)
    return pl.pallas_call(
        weights_kernel,
        grid_spec=pltpu.PrefetchScalarGridSpec(
            num_scalar_prefetch=1,
            grid=(4,),
            in_specs=[tile, tile],
            out_specs=pl.BlockSpec((size, size), out_at),
        ),
        out_shape=jax.ShapeDtypeStruct((2 * size, 2 * size), stored.dtype),
        cost_estimate=pl.CostEstimate(flops=8 * size * size, bytes_accessed=24 * size * size, transcendentals=0),
        name="dense_weights",
    )(slots, stored, noise)


def grads_kernel(down, n_left, n_own, slots, place_of, *refs):
    lefts, owns, others = refs[:n_left], refs[n_left : n_left + n_own], refs[n_left + n_own : -5]
    noise, out, left, right, sems = refs[-5:]
    s = pl.program_id(0)
    size, width, rows = out.shape[1], left.shape[-1], left.shape[-2]
    tk = others[0].shape[-2]
    core, x, y = place_of[0], place_of[1], place_of[2]
    place = slots[s]
    hidden = pl.ds(pl.multiple_of((place & 1) * size, size), size)
    feature = pl.ds(pl.multiple_of((place >> 1) * size, size), size)
    a, b = (hidden, feature) if down else (feature, hidden)

    def line_at(array, half, from_core, d):
        return array.at[half, :, (y + d) & 3] if from_core == 0 else array.at[half, (x + d) & 3]

    def copies(me, half):
        pairs = []
        if down:
            for source, of in zip(lefts, (me, 1 - me)):
                pairs.append((source.at[:, :, half], left.at[half, :, pl.ds(2 * of, 2)]))
        else:
            for d, source in enumerate(lefts):
                pairs.append((source.at[:, half], line_at(left, half, me, d)))
        for k in range(2):
            for d in range(4):
                if half == me:
                    source = owns[4 * k + d].at[:, :, pl.ds(0, width)] if down else owns[k].at[d]
                else:
                    source = others[0].at[k, d] if len(others) == 1 else others[k].at[d]
                pairs.append((source, line_at(right, half, half, d).at[:, pl.ds(k * tk, tk)]))
        first = half * 12
        return [pltpu.make_async_copy(*pair, sems.at[first + i]) for i, pair in enumerate(pairs)]

    @pl.when(s == 0)
    def _():
        for me in range(2):

            @pl.when(core == me)
            def _():
                for half in range(2):
                    for copy in copies(me, half):
                        copy.start()

    for half in range(2):

        @pl.when(s == 0)
        def _():
            for me in range(2):

                @pl.when(core == me)
                def _():
                    for copy in copies(me, half):
                        copy.wait()

            if down:

                @pl.loop(0, 16)
                def _(i):
                    wide = left[half, i >> 2, i & 3].astype(jnp.float32)
                    left[half, i >> 2, i & 3] = (wide * jax.nn.sigmoid(wide)).astype(left.dtype)

        @pl.when(place >= 0)
        def _():
            rows_first = (((0,), (0,)), ((), ()))
            more = lax.dot_general(
                left[half, :, :, :, a].reshape(16 * rows, size),
                right[half, :, :, :, b].reshape(16 * rows, size),
                rows_first,
                preferred_element_type=jnp.float32,
            )
            if half == 0:
                out[0] = more
            else:
                out[0] = (more + out[0]) * (1.0 + noise[0].astype(jnp.float32))

    @pl.when(place < 0)
    def _():
        out[...] = jnp.zeros_like(out)


def slot_grads(slots, place_of, lefts, owns, others, noise, down):
    rows, width = lefts[0].shape[-2:]
    size = noise.shape[-1]
    tile = pl.BlockSpec((1, size, size), lambda s, *_: (s, 0, 0))
    anywhere = pl.BlockSpec(memory_space=pl.ANY)
    whole = pltpu.VMEM((2, 4, 4, rows, width), noise.dtype)
    return pl.pallas_call(
        functools.partial(grads_kernel, down, len(lefts), len(owns)),
        grid_spec=pltpu.PrefetchScalarGridSpec(
            num_scalar_prefetch=2,
            grid=(4,),
            in_specs=[anywhere] * (len(lefts) + len(owns) + len(others)) + [tile],
            out_specs=tile,
            scratch_shapes=[whole, whole, pltpu.SemaphoreType.DMA((24,))],
        ),
        out_shape=jax.ShapeDtypeStruct(noise.shape, jnp.float32),
        compiler_params=pltpu.CompilerParams(vmem_limit_bytes=GRADS_VMEM),
        cost_estimate=pl.CostEstimate(
            flops=8 * 32 * rows * size * size, bytes_accessed=14 * 2**20, transcendentals=0
        ),
        name="slot_grads",
    )(slots, place_of, *lefts, *owns, *others, noise)


def dot(a, b, contract, kind):
    return lax.dot_general(a, b, (contract, ((), ())), preferred_element_type=jnp.float32).astype(kind)


def add_up(parts):
    total = parts[0].astype(jnp.float32)
    for part in parts[1:]:
        total = total + part.astype(jnp.float32)
    return total


def on_device(inputs, grad_out, pre_act, up_w, up_noise, down_w, down_noise, up_slot, down_slot):
    z, c, x, y = (lax.axis_index(a).astype(jnp.uint32) for a in ("z", "c", "x", "y"))
    first, second = jnp.where(c == 0, x, y), jnp.where(c == 0, y, x)
    other_c = c ^ jnp.uint32(1)
    ahead = lambda index, d: (index + jnp.asarray(d, jnp.uint32)) & jnp.uint32(3)
    bf16 = jnp.bfloat16
    rows, feats = grad_out.shape
    hidden = pre_act.shape[1]
    half = rows // 2
    tk = half // 2
    up_slots, down_slots = up_slot[0], down_slot[0]
    place_of = jnp.stack([c, x, y]).astype(jnp.int32)

    def down_product(dy):
        return dot(dy.reshape(-1, 2 * feats), down_both, ((1,), (1,)), bf16).reshape(4, -1, hidden)

    def up_product(hg):
        return dot(hg.reshape(-1, hidden), up_both, ((1,), (1,)), bf16).reshape(4, 4, tk, 2 * feats)

    def sum_of_four(parts):
        return add_up([parts[i] for i in range(4)])

    def pieces_of(line):
        return [plane(-d, line) for d in (1, 2, 3)]

    def line_of(pieces):
        line = jnp.zeros((4,) + pieces[0].shape, bf16)
        for d, piece in enumerate(pieces):
            line = put(line, piece[None], (ahead(first, d), 0, 0))
        return line

    halves, other_halves = (rows_of.reshape(2, half, feats) for rows_of in (grad_out, swap(grad_out)))
    here = jnp.concatenate([take(halves, c), take(other_halves, c), inputs], 0)
    down_own = dense_weights(down_slots, after(down_w, here)[0], down_noise[0], True)
    near = [here] + [after(along(-d, here, True), down_own) for d in (1, 2, 3)]
    both = lambda piece, cut: jnp.concatenate([piece[:half][cut], piece[half:rows][cut]], 1)
    line_a = line_of([both(piece, slice(0, tk)) for piece in near])
    line_b = line_of([both(piece, slice(tk, half)) for piece in near])
    line_x = line_of([after(piece, line_a)[rows:] for piece in near])

    h_own = exchange_z(four(after(pre_act, here))).reshape(4, 2, 2, half, hidden)
    down_both = jnp.concatenate([down_own, swap(down_own)], 1)

    up_own = dense_weights(up_slots, after(up_w, line_a)[0], up_noise[0], False)
    pieces_a = [line_a, *pieces_of(line_a)]
    dy_a = jnp.stack(pieces_a)
    partial_a = down_product(after(dy_a, line_x, up_own))

    parts_a = exchange_z(after(partial_a, h_own))
    up_both = jnp.concatenate([up_own, swap(up_own)], 0)

    h_other = swap(after(h_own, partial_a))
    h_here = after(h_own, h_other)
    at = ahead(second, z)
    near = at < jnp.uint32(2)
    on_0 = jnp.where(near, take(h_here, at & jnp.uint32(1), 1)[:, 0], take(h_other, at & jnp.uint32(1), 1)[:, 0])
    on_1 = jnp.concatenate([take(h_other, at)[:, 1], take(h_here, at)[:, 1]], 0)
    h_mine = jnp.where(c == 0, on_0, on_1)

    def hidden_grad(parts, k):
        return (sum_of_four(parts) * slopes[k].reshape(4 * tk, hidden)).astype(bf16)

    slopes = silu_slope(h_mine)
    slopes = lax.optimization_barrier([slopes[:, :tk], slopes[:, tk:]])

    other_a = swap(jnp.stack([after(piece, h_other)[..., feats:] for piece in pieces_a]))
    hg_a = hidden_grad(after(parts_a, other_a, *slopes), 0)
    line_b = after(line_b, h_other, *pieces_a)
    pieces_b = [line_b, *pieces_of(line_b)]
    dy_b = jnp.stack(pieces_b)
    other_b = swap(dy_b[..., feats:])
    partial_b = down_product(dy_b)
    sent_b = after(partial_b, other_b)
    parts_b = [take(partial_b, z)]
    for d in (1, 2, 3):
        parts_b.append(lax.ppermute(take(sent_b, ahead(z, d)), "z", [(i, (i + d) % 4) for i in range(4)]))
    sent_hg = four(hg_a)
    all_a = after(exchange_z(sent_hg), partial_b)

    line_x = in_turn(line_x, sent_hg)
    x_1, x_3 = plane(-1, line_x), plane(-3, line_x)
    x_2 = plane(-2, after(line_x, x_1, x_3))
    down_grad = slot_grads(
        down_slots, place_of, [h_own, h_other], pieces_a + pieces_b, [other_a, other_b], down_noise[0], True
    )
    hg_b = hidden_grad([after(parts_b[0], all_a, down_grad)] + parts_b[1:], 1)
    out_a = up_product(after(all_a, hg_b))
    own_a, *sent_a = lax.optimization_barrier([out_a[d] for d in range(4)])
    sum_a = add_up([own_a] + [plane(d, sent_a[d - 1]) for d in (1, 2, 3)]).astype(bf16)
    hgs = [hg.reshape(4, 4, tk, hidden) for hg in (all_a, exchange_z(four(hg_b)))]
    other_hg = swap(hgs[0])
    all_b = after(hgs[1], other_hg, x_2, *sent_a)
    out_b = up_product(all_b)
    own_b, *sent_b = lax.optimization_barrier([out_b[d] for d in range(4)])
    x_lines = [line_x.reshape(4, 2, half, feats) for line_x in (line_x, x_1, x_2, x_3)]
    up_grad = slot_grads(up_slots, place_of, x_lines, [hgs[0], all_b], [other_hg, swap(all_b)], up_noise[0], False)
    sum_b = add_up([own_b] + [after(plane(d, sent_b[d - 1]), up_grad) for d in (1, 2, 3)]).astype(bf16)
    summed = exchange_first(jnp.concatenate([sum_a, sum_b], 1))
    mine = sum_of_four(summed).astype(bf16)
    input_grad = jnp.zeros((2, half, feats), bf16)
    input_grad = put(input_grad, mine[None, :, :feats], (c, 0, 0))
    input_grad = put(input_grad, swap(mine[:, feats:])[None], (other_c, 0, 0))
    return input_grad.reshape(rows, feats), up_grad[None], down_grad[None]


def solution(mesh):
    fine = Mesh(mesh.devices.reshape(4, 2, 4, 4), ("z", "c", "x", "y"))
    row, col = ("z", "c"), ("x", "y")
    in_specs = (P(col, row), P(col, row), P(row, col)) + (P(row, col),) * 6
    out_specs = (P(col, row), P(row, col), P(row, col))
    return jax.shard_map(
        on_device, mesh=fine, in_specs=in_specs, out_specs=out_specs, check_vma=False
    )
```
